32 devices in a mesh: dp: 8 (over z, core), tensor: 2 (over y), mp: 2 (over x).
Axes of the slice: x: 2, y: 2, z: 4, core: 2. Of those that a mesh axis runs over, the one named last changes fastest.
Arguments:
- step_embeds: bfloat16 [2, 256, 32, 8192], P('mp', 'dp', None, 'tensor'), may hold values from -6 to 6
- step_len: int32 [256], replicated, may hold values from 8 to 32, as said below
- leaf_of_step: int32 [256], replicated, may hold values from 0 to 31, as said below
- cache_len: int32 [32], P('dp'), may hold values from 96 to 768, as said below
- caches: bfloat16 [2, 32, 768, 2048], P('mp', 'dp', None, 'tensor'), may hold values from -500 to 500
- norm_gain: float32 [2, 8192], P('mp'), may hold values from 0.1 to 1.9
- qkv_weight: bfloat16 [2, 8192, 6144], P('mp', 'dp', 'tensor'), may hold values from -0.1875 to 0.1875
- score_weight: float32 [2, 4096], P('mp', 'tensor'), may hold values from -0.09375 to 0.09375
Outputs:
- contexts: bfloat16 [2, 32, 8, 32, 4096], P('mp', 'dp', None, None, 'tensor')
- step_value: float32 [32, 8], P('dp')
The draws below stay inside these ranges and needn't reach their ends.
Inputs may be any that keep to these rules, and one draw needn't show every extreme that they name: `leaf_of_step`: every leaf is named by exactly 8 steps, and each aligned block of 32 steps names the leaves of every aligned block of 4 leaves equally often. `step_len`: some step has all 32 tokens. `cache_len`: some leaf fills all 768 cache positions.
All inputs are finite; a program needn't handle non-finite values.
Results may differ from the reference program's by a relative error of at most 0.0049.
The reference program's roundings to bfloat16 on the way count: a program that leaves them out, or rounds other values in their place, can miss the bound.
Values may be sent and summed in bfloat16 or wider, within the bound.
A program may use at most 192 MiB of HBM per device.

```python
import jax
import jax.numpy as jnp
from jax import lax

D = 8192
KVH = 8
HD = 128
HQ = 32
SPL = 8
SMAX = 32
CTX = 768
LEAF_DEV = 4
QKV = 6144
STEP_DEV = 32
LEAVES = 32
STEPS = 256


def draw_leaf_of_step(key, part):
    part_count = STEPS // STEP_DEV
    per_peer = STEP_DEV // part_count
    send_keys = jax.random.split(jax.random.fold_in(key, 11), part_count)
    slot_of = jax.vmap(lambda sub_key: jax.random.permutation(sub_key, STEP_DEV))(send_keys)
    owner = slot_of // per_peer
    incoming = jnp.arange(part_count, dtype=jnp.int32)[:, None] * per_peer + slot_of % per_peer
    recv_keys = jax.random.split(jax.random.fold_in(key, 12), part_count)
    seating = jax.vmap(lambda sub_key: jax.random.permutation(sub_key, STEP_DEV))(recv_keys)
    seat_of = seating[owner, incoming]
    leaves = owner * LEAF_DEV + seat_of // SPL
    return leaves.reshape(STEPS).astype(jnp.int32)


def draw_step_len(key, part):
    drawn = jax.random.randint(jax.random.fold_in(key, 21), (STEPS,), SMAX // 4, SMAX + 1)
    chosen = jax.random.randint(jax.random.fold_in(key, 22), (), 0, STEPS)
    return jnp.where(jnp.arange(STEPS) == chosen, SMAX, drawn).astype(jnp.int32)


def draw_cache_len(key, part):
    drawn = jax.random.randint(jax.random.fold_in(key, 23), (LEAVES,), CTX // 8, CTX + 1)
    chosen = jax.random.randint(jax.random.fold_in(key, 24), (), 0, LEAVES)
    return jnp.where(jnp.arange(LEAVES) == chosen, CTX, drawn).astype(jnp.int32)


def draw_caches(key, part):
    array_shape = (2, LEAVES, CTX, 2 * KVH * HD)
    drawn = jax.random.normal(jax.random.fold_in(key, 35), array_shape, jnp.float32)
    return jnp.clip(drawn, -6.0, 6.0).astype(jnp.bfloat16)


def level_of(rng, shape, cuts, smallest, high):
    factor_of = 1.0
    for dim, shards_of in cuts:
        heights = jax.random.uniform(jax.random.fold_in(jax.random.fold_in(rng, 6), dim), (shards_of,), jnp.float32, smallest / len(cuts), high / len(cuts))
        factor_of = factor_of * jnp.repeat(jnp.exp(heights), shape[dim] // shards_of).reshape((-1,) + (1,) * (len(shape) - 1 - dim))
    return factor_of


def gaussian(rng, extent, scale, reach, cuts=(), kind=jnp.bfloat16):
    loudness = level_of(rng, extent, cuts, -0.22, 0.18) if cuts else 1.0
    result = jax.random.normal(rng, extent, jnp.float32) * scale * loudness
    return jnp.minimum(jnp.maximum(result, -reach), reach).astype(kind)


def setup_inputs(seed: int = 0) -> dict:
    keys = jax.random.split(jax.random.key(seed), 9)
    return {
        "step_embeds": gaussian(keys[0], (2, STEPS, SMAX, D), 1.0, 6.0, ((0, 2), (1, 8), (3, 2))),
        "step_len": draw_step_len(jax.random.fold_in(keys[8], 71), 0),
        "leaf_of_step": draw_leaf_of_step(jax.random.fold_in(keys[8], 71), 0),
        "cache_len": draw_cache_len(jax.random.fold_in(keys[8], 71), 0),
        "caches": draw_caches(jax.random.fold_in(keys[8], 71), 0),
        "norm_gain": jnp.clip(1.0 + 0.18 * jax.random.normal(keys[5], (2, D), jnp.float32), 0.1, 1.9),
        "qkv_weight": gaussian(keys[6], (2, D, QKV), (D // 8) ** -0.5, 0.1875, ((0, 2), (1, 8), (2, 2))),
        "score_weight": gaussian(keys[7], (2, HQ * HD), (HQ * HD) ** -0.5, 0.09375, ((0, 2), (1, 2)), jnp.float32),
    }


prior_weight = 0.5
norm_eps = 1e-05

def one_model(embeds, lengths, cache_lens, cache, gain, weight, score_vec, order):
    group_size = HQ // KVH

    def per_leaf(inputs):
        leaf_steps, leaf_cache, leaf_len = inputs
        rows = embeds[leaf_steps]
        step_lens = lengths[leaf_steps]
        as_float = rows.astype(jnp.float32)
        inverse_rms = lax.rsqrt(lax.optimization_barrier(jnp.mean(as_float * as_float, axis=-1, keepdims=True)) + norm_eps)
        normed = (as_float * inverse_rms * gain).astype(jnp.bfloat16)
        projected = jnp.dot(normed.reshape(SPL * SMAX, D), weight, preferred_element_type=jnp.float32).astype(jnp.bfloat16)
        projected = projected.reshape(SPL, SMAX, KVH, group_size + 2, HD)
        queries = projected[:, :, :, :group_size].astype(jnp.float32)
        key_own = projected[:, :, :, group_size].astype(jnp.float32)
        value_own = projected[:, :, :, group_size + 1].astype(jnp.float32)
        cache_rows = leaf_cache.reshape(CTX, KVH, 2, HD)
        key_cache = cache_rows[:, :, 0].astype(jnp.float32)
        value_cache = cache_rows[:, :, 1].astype(jnp.float32)
        scale_q = HD ** (-0.5)
        own_scores = jnp.einsum('sikgh,sjkh->sikgj', queries, key_own) * scale_q
        positions = jnp.arange(SMAX, dtype=jnp.int32)
        causal = positions[None, :] <= positions[:, None]
        own_scores = jnp.where(causal[:, None, None, :], own_scores, -jnp.inf)
        far_scores = jnp.einsum('sikgh,ckh->sikgc', queries, key_cache) * scale_q
        is_live = jnp.arange(CTX, dtype=jnp.int32) < leaf_len
        far_scores = jnp.where(is_live, far_scores, -jnp.inf)
        row_max = jnp.maximum(own_scores.max(-1), far_scores.max(-1))
        own_probs = jnp.exp(own_scores - row_max[..., None])
        far_probs = jnp.exp(far_scores - row_max[..., None])
        total = own_probs.sum(-1) + far_probs.sum(-1)
        own_b = own_probs.astype(jnp.bfloat16).astype(jnp.float32)
        far_b = far_probs.astype(jnp.bfloat16).astype(jnp.float32)
        context = jnp.einsum('sikgj,sjkh->sikgh', own_b, value_own) + jnp.einsum('sikgc,ckh->sikgh', far_b, value_cache)
        context = context / total[..., None]
        is_valid = positions[None, :] < step_lens[:, None]
        context = jnp.where(is_valid[:, :, None, None, None], context, 0.0)
        flat = context.reshape(SPL, SMAX, HQ * HD)
        last_token = (positions[None, :] == step_lens[:, None] - 1).astype(jnp.float32)
        last_context = lax.optimization_barrier(jnp.sum(last_token[:, :, None] * flat, axis=1))
        score = lax.optimization_barrier(jnp.sum(last_context * score_vec, axis=-1))
        return (flat.astype(jnp.bfloat16), score)
    return lax.map(per_leaf, (order, cache, cache_lens))

def reference(step_embeds, step_len, leaf_of_step, cache_len, caches, norm_gain, qkv_weight, score_weight):
    step_index = jnp.arange(STEPS, dtype=jnp.int32)
    order = jnp.argsort(leaf_of_step * STEPS + step_index).astype(jnp.int32).reshape(LEAVES, SPL)
    policy_ctx, policy_score = one_model(step_embeds[0], step_len, cache_len, caches[0], norm_gain[0], qkv_weight[0], score_weight[0], order)
    reward_ctx, reward_score = one_model(step_embeds[1], step_len, cache_len, caches[1], norm_gain[1], qkv_weight[1], score_weight[1], order)
    contexts = jnp.stack([policy_ctx, reward_ctx], axis=0)
    step_value = prior_weight * policy_score + reward_score
    return (contexts, step_value)
```

```python
import functools

import jax
import jax.numpy as jnp
from jax import lax
from jax.experimental import pallas as pl
from jax.experimental.pallas import tpu as pltpu
from jax.sharding import PartitionSpec as P

KVH = 8
HD = 128
HQ = 32


prior_weight = 0.5
norm_eps = 1e-05


def permute_kernel(order_ref, rows_ref, out_ref):
    def move(slot, carry):
        out_ref[slot] = rows_ref[order_ref[slot]]
        return carry

    lax.fori_loop(0, out_ref.shape[0], move, 0)


def permute_steps(order, rows):
    size = rows.size * rows.dtype.itemsize
    return pl.pallas_call(
        permute_kernel,
        out_shape=jax.ShapeDtypeStruct(rows.shape, rows.dtype),
        in_specs=[
            pl.BlockSpec(memory_space=pltpu.SMEM),
            pl.BlockSpec(memory_space=pltpu.VMEM),
        ],
        out_specs=pl.BlockSpec(memory_space=pltpu.VMEM),
        compiler_params=pltpu.CompilerParams(vmem_limit_bytes=2 * size + (4 << 20)),
        cost_estimate=pl.CostEstimate(flops=0, bytes_accessed=2 * size, transcendentals=0),
    )(order, rows)


def attend_kernel(
    per_leaf,
    group_size,
    arrange_ref,
    length_ref,
    live_ref,
    rows_ref,
    cache_ref,
    weight_ref,
    *refs,
):
    out_ref, score_ref, query_s, key_s, value_s = refs[-5:]
    leaf = pl.program_id(0)
    seq_max = rows_ref.shape[1]
    cache_rows = cache_ref.shape[2]
    steps_tile = query_s.shape[1] // seq_max
    tile = steps_tile * seq_max
    keys = cache_rows + tile
    key_s[:cache_rows] = cache_ref[0, 0, :, :HD]
    value_s[:cache_rows] = cache_ref[0, 0, :, HD:]
    row = lax.broadcasted_iota(jnp.int32, (tile, keys), 0)
    column = lax.broadcasted_iota(jnp.int32, (tile, keys), 1)
    own = column - cache_rows
    first = row - lax.rem(row, seq_max)
    far_ok = column < jnp.minimum(live_ref[leaf], cache_rows)
    own_ok = (own >= first) & (own <= row)
    bias = jnp.where(far_ok | own_ok, 0.0, -jnp.inf)
    token = lax.broadcasted_iota(jnp.int32, (seq_max, HD), 0)
    scale_q = HD ** (-0.5)
    for part in range(per_leaf // steps_tile):
        valid, last = [], []
        for place in range(steps_tile):
            slot = leaf * per_leaf + part * steps_tile + place
            step = arrange_ref[slot]
            span = pl.ds(place * seq_max, seq_max)
            for head in range(group_size):
                query_s[head, span] = rows_ref[step, :, head * HD : (head + 1) * HD]
            key_s[pl.ds(cache_rows + place * seq_max, seq_max)] = rows_ref[
                step, :, group_size * HD : (group_size + 1) * HD
            ]
            value_s[pl.ds(cache_rows + place * seq_max, seq_max)] = rows_ref[
                step, :, (group_size + 1) * HD : (group_size + 2) * HD
            ]
            valid.append(token < length_ref[slot])
            last.append((token == length_ref[slot] - 1).astype(jnp.float32))
        step_score = [jnp.zeros((1, HD), jnp.float32) for _ in range(steps_tile)]
        for head in range(group_size):
            scores = lax.dot_general(
                query_s[head],
                key_s[...],
                (((1,), (1,)), ((), ())),
                preferred_element_type=jnp.float32,
            )
            scores = scores * scale_q + bias
            probs = jnp.exp(scores - scores.max(-1, keepdims=True))
            total = probs.sum(-1, keepdims=True)
            context = jnp.dot(
                probs.astype(jnp.bfloat16), value_s[...], preferred_element_type=jnp.float32
            )
            context = context / total
            for place in range(steps_tile):
                piece = jnp.where(
                    valid[place], context[place * seq_max : (place + 1) * seq_max], 0.0
                )
                out_ref[0, 0, part * steps_tile + place, :, head * HD : (head + 1) * HD] = (
                    piece.astype(jnp.bfloat16)
                )
                step_score[place] += (piece * last[place]).sum(0, keepdims=True) * weight_ref[
                    :, head * HD : (head + 1) * HD
                ]
        for place in range(steps_tile):
            score_ref[0, pl.ds(part * steps_tile + place, 1)] = step_score[place]


def attend(group, groups, per_leaf, arrange, lengths, live, rows, caches, weight, contexts):
    steps_here, seq_max, columns = rows.shape
    _, leaves_here, cache_rows, _ = caches.shape
    group_size = HQ // KVH
    tile = 128
    width = group_size * HD
    in_specs = [
        pl.BlockSpec((steps_here, seq_max, columns), lambda l, *_: (0, 0, 0)),
        pl.BlockSpec((1, 1, cache_rows, 2 * HD), lambda l, *_: (0, l, 0, group)),
        pl.BlockSpec((1, width), lambda l, *_: (0, group)),
    ]
    operands = [rows, caches, weight]
    aliases = {}
    if contexts is not None:
        in_specs.append(pl.BlockSpec(memory_space=pl.ANY))
        operands.append(contexts)
        aliases = {6: 0}
    work = steps_here * seq_max * group_size * (cache_rows + tile)
    return pl.pallas_call(
        functools.partial(attend_kernel, per_leaf, group_size),
        grid_spec=pltpu.PrefetchScalarGridSpec(
            num_scalar_prefetch=3,
            grid=(leaves_here,),
            in_specs=in_specs,
            out_specs=[
                pl.BlockSpec(
                    (1, 1, per_leaf, seq_max, width), lambda l, *_: (0, l, 0, 0, group)
                ),
                pl.BlockSpec((1, per_leaf, HD), lambda l, *_: (l, 0, 0)),
            ],
            scratch_shapes=[
                pltpu.VMEM((group_size, tile, HD), jnp.bfloat16),
                pltpu.VMEM((cache_rows + tile, HD), jnp.bfloat16),
                pltpu.VMEM((cache_rows + tile, HD), jnp.bfloat16),
            ],
        ),
        out_shape=[
            jax.ShapeDtypeStruct(
                (1, leaves_here, per_leaf, seq_max, groups * width), jnp.bfloat16
            ),
            jax.ShapeDtypeStruct((leaves_here, per_leaf, HD), jnp.float32),
        ],
        input_output_aliases=aliases,
        compiler_params=pltpu.CompilerParams(vmem_limit_bytes=24 << 20),
        cost_estimate=pl.CostEstimate(
            flops=4 * work * HD, bytes_accessed=8 << 20, transcendentals=work
        ),
    )(arrange, lengths, live, *operands)


def per_device(
    step_embeds, step_len, leaf_of_step, cache_len, caches, norm_gain, qkv_weight, score_weight
):
    embeds = step_embeds[0]
    steps_here, seq_max, piece_width = embeds.shape
    row_width = norm_gain.shape[1]
    leaves_here = cache_len.shape[0]
    per_leaf = steps_here // leaves_here
    groups = caches.shape[3] // (2 * HD)
    group_size = HQ // KVH
    part_count = lax.axis_size("dp")
    dp_index = lax.axis_index("dp")
    tensor_count = lax.axis_size("tensor")
    tensor_index = lax.axis_index("tensor")
    per_peer = steps_here // part_count
    total_steps = leaf_of_step.shape[0]

    own = embeds.reshape(steps_here * seq_max, piece_width)
    width = (group_size + 2) * HD
    gathered = [
        lax.all_gather(
            qkv_weight[0, :, g * width : (g + 1) * width], "dp", axis=0, tiled=True
        )
        for g in range(groups)
    ]
    local_rows = jnp.zeros((steps_here * seq_max, row_width), own.dtype)
    for shift in range(tensor_count):
        source = lax.rem(tensor_index + tensor_count - shift, tensor_count)
        piece = own
        if shift:
            hops = [(i, (i + shift) % tensor_count) for i in range(tensor_count)]
            piece = lax.ppermute(own, "tensor", hops)
        local_rows = lax.dynamic_update_slice_in_dim(
            local_rows, piece, source * piece_width, 1
        )

    local_ids = jnp.arange(steps_here, dtype=jnp.int32)
    owners = (leaf_of_step // leaves_here).reshape(part_count, steps_here)
    send_orders = jnp.argsort(owners * steps_here + local_ids[None, :], axis=1)
    send_order = lax.dynamic_index_in_dim(send_orders, dp_index, 0, keepdims=False)
    sources = jnp.arange(part_count, dtype=jnp.int32)[:, None] * steps_here
    arriving = (
        lax.dynamic_slice_in_dim(send_orders, dp_index * per_peer, per_peer, 1) + sources
    ).reshape(steps_here)
    arrive_leaf = leaf_of_step[arriving] - dp_index * leaves_here
    arrange = jnp.argsort(arrive_leaf * total_steps + arriving).astype(jnp.int32)
    lengths = step_len[arriving[arrange]]

    as_float = local_rows.astype(jnp.float32)
    inverse_rms = lax.rsqrt(jnp.mean(as_float * as_float, axis=-1, keepdims=True) + norm_eps)
    normed = (as_float * inverse_rms * norm_gain[0]).astype(jnp.bfloat16)

    contexts, partial_value = None, 0.0
    for g in range(groups):
        summed = jnp.dot(normed, gathered[g], preferred_element_type=jnp.float32)
        outbound = summed.astype(jnp.bfloat16).reshape(steps_here, seq_max, width)
        outbound = permute_steps(send_order, outbound)
        outbound = outbound.reshape(part_count, per_peer, seq_max, width)
        arrived = lax.all_to_all(outbound, "dp", split_axis=0, concat_axis=0, tiled=True)
        arrived = arrived.reshape(steps_here, seq_max, width)
        contexts, shares = attend(
            g, groups, per_leaf, arrange, lengths, cache_len, arrived, caches, score_weight, contexts
        )
        partial_value = partial_value + jnp.sum(shares, axis=-1)
    model_weight = jnp.where(lax.axis_index("mp") == 0, prior_weight, 1.0).astype(jnp.float32)
    step_value = lax.psum(partial_value * model_weight, ("tensor", "mp"))
    return (contexts, step_value)


def solution(mesh):
    placed = (
        P("mp", "dp", None, "tensor"),
        P(),
        P(),
        P("dp"),
        P("mp", "dp", None, "tensor"),
        P("mp", None),
        P("mp", "dp", "tensor"),
        P("mp", "tensor"),
    )
    return jax.shard_map(
        per_device,
        mesh=mesh,
        in_specs=placed,
        out_specs=(P("mp", "dp", None, None, "tensor"), P("dp", None)),
        check_vma=False,
    )
```

```python
import functools

import jax
import jax.numpy as jnp
from jax import lax
from jax.experimental import pallas as pl
from jax.experimental.pallas import tpu as pltpu
from jax.sharding import PartitionSpec as P

KVH = 8
HD = 128
HQ = 32


prior_weight = 0.5
norm_eps = 1e-05


def permute_kernel(order_ref, rows_ref, *refs):
    out_ref = refs[-1]

    def move(slot, carry):
        out_ref[slot] = rows_ref[order_ref[slot]]
        return carry

    lax.fori_loop(0, out_ref.shape[0], move, 0)


def permute_steps(order, rows, after):
    size = rows.size * rows.dtype.itemsize
    return pl.pallas_call(
        permute_kernel,
        out_shape=jax.ShapeDtypeStruct(rows.shape, rows.dtype),
        in_specs=[
            pl.BlockSpec(memory_space=pltpu.SMEM),
            pl.BlockSpec(memory_space=pltpu.VMEM),
        ]
        + [pl.BlockSpec(memory_space=pl.ANY)] * len(after),
        out_specs=pl.BlockSpec(memory_space=pltpu.VMEM),
        compiler_params=pltpu.CompilerParams(vmem_limit_bytes=2 * size + (4 << 20)),
        cost_estimate=pl.CostEstimate(flops=0, bytes_accessed=2 * size, transcendentals=0),
    )(order, rows, *after)


def attend_kernel(
    per_leaf,
    group_size,
    arrange_ref,
    length_ref,
    live_ref,
    rows_ref,
    cache_ref,
    weight_ref,
    *refs,
):
    out_ref, score_ref, query_s, key_s, value_s = refs[-5:]
    leaf = pl.program_id(0)
    seq_max = rows_ref.shape[1]
    cache_rows = cache_ref.shape[2]
    steps_tile = query_s.shape[1] // seq_max
    tile = steps_tile * seq_max
    keys = cache_rows + tile
    key_s[:cache_rows] = cache_ref[0, 0, :, :HD]
    value_s[:cache_rows] = cache_ref[0, 0, :, HD:]
    row = lax.broadcasted_iota(jnp.int32, (tile, keys), 0)
    column = lax.broadcasted_iota(jnp.int32, (tile, keys), 1)
    own = column - cache_rows
    first = row - lax.rem(row, seq_max)
    far_ok = column < jnp.minimum(live_ref[leaf], cache_rows)
    own_ok = (own >= first) & (own <= row)
    bias = jnp.where(far_ok | own_ok, 0.0, -jnp.inf)
    token = lax.broadcasted_iota(jnp.int32, (seq_max, HD), 0)
    scale_q = HD ** (-0.5)
    for part in range(per_leaf // steps_tile):
        valid, last = [], []
        for place in range(steps_tile):
            slot = leaf * per_leaf + part * steps_tile + place
            step = arrange_ref[slot]
            span = pl.ds(place * seq_max, seq_max)
            for head in range(group_size):
                query_s[head, span] = rows_ref[step, :, head * HD : (head + 1) * HD]
            key_s[pl.ds(cache_rows + place * seq_max, seq_max)] = rows_ref[
                step, :, group_size * HD : (group_size + 1) * HD
            ]
            value_s[pl.ds(cache_rows + place * seq_max, seq_max)] = rows_ref[
                step, :, (group_size + 1) * HD : (group_size + 2) * HD
            ]
            valid.append(token < length_ref[slot])
            last.append((token == length_ref[slot] - 1).astype(jnp.float32))
        step_score = [jnp.zeros((1, HD), jnp.float32) for _ in range(steps_tile)]
        for head in range(group_size):
            scores = lax.dot_general(
                query_s[head],
                key_s[...],
                (((1,), (1,)), ((), ())),
                preferred_element_type=jnp.float32,
            )
            scores = scores * scale_q + bias
            probs = jnp.exp(scores - scores.max(-1, keepdims=True))
            total = probs.sum(-1, keepdims=True)
            context = jnp.dot(
                probs.astype(jnp.bfloat16), value_s[...], preferred_element_type=jnp.float32
            )
            context = context / total
            for place in range(steps_tile):
                piece = jnp.where(
                    valid[place], context[place * seq_max : (place + 1) * seq_max], 0.0
                )
                out_ref[0, 0, part * steps_tile + place, :, head * HD : (head + 1) * HD] = (
                    piece.astype(jnp.bfloat16)
                )
                step_score[place] += (piece * last[place]).sum(0, keepdims=True) * weight_ref[
                    :, head * HD : (head + 1) * HD
                ]
        for place in range(steps_tile):
            score_ref[0, pl.ds(part * steps_tile + place, 1)] = step_score[place]


def attend(group, groups, per_leaf, arrange, lengths, live, rows, caches, weight, contexts):
    steps_here, seq_max, columns = rows.shape
    _, leaves_here, cache_rows, _ = caches.shape
    group_size = HQ // KVH
    tile = 128
    width = group_size * HD
    in_specs = [
        pl.BlockSpec((steps_here, seq_max, columns), lambda l, *_: (0, 0, 0)),
        pl.BlockSpec((1, 1, cache_rows, 2 * HD), lambda l, *_: (0, l, 0, group)),
        pl.BlockSpec((1, width), lambda l, *_: (0, group)),
    ]
    operands = [rows, caches, weight]
    aliases = {}
    if contexts is not None:
        in_specs.append(pl.BlockSpec(memory_space=pl.ANY))
        operands.append(contexts)
        aliases = {6: 0}
    work = steps_here * seq_max * group_size * (cache_rows + tile)
    return pl.pallas_call(
        functools.partial(attend_kernel, per_leaf, group_size),
        grid_spec=pltpu.PrefetchScalarGridSpec(
            num_scalar_prefetch=3,
            grid=(leaves_here,),
            in_specs=in_specs,
            out_specs=[
                pl.BlockSpec(
                    (1, 1, per_leaf, seq_max, width), lambda l, *_: (0, l, 0, 0, group)
                ),
                pl.BlockSpec((1, per_leaf, HD), lambda l, *_: (l, 0, 0)),
            ],
            scratch_shapes=[
                pltpu.VMEM((group_size, tile, HD), jnp.bfloat16),
                pltpu.VMEM((cache_rows + tile, HD), jnp.bfloat16),
                pltpu.VMEM((cache_rows + tile, HD), jnp.bfloat16),
            ],
        ),
        out_shape=[
            jax.ShapeDtypeStruct(
                (1, leaves_here, per_leaf, seq_max, groups * width), jnp.bfloat16
            ),
            jax.ShapeDtypeStruct((leaves_here, per_leaf, HD), jnp.float32),
        ],
        input_output_aliases=aliases,
        compiler_params=pltpu.CompilerParams(vmem_limit_bytes=24 << 20),
        cost_estimate=pl.CostEstimate(
            flops=4 * work * HD, bytes_accessed=8 << 20, transcendentals=work
        ),
    )(arrange, lengths, live, *operands)


def sum_over(value, axis):
    count = lax.axis_size(axis)
    if count & (count - 1):
        return lax.psum(value, axis)
    reach = 1
    while reach < count:
        hops = [(i, i ^ reach) for i in range(count)]
        value = value + lax.ppermute(value, axis, hops)
        reach *= 2
    return value


def per_device(
    step_embeds, step_len, leaf_of_step, cache_len, caches, norm_gain, qkv_weight, score_weight
):
    embeds = step_embeds[0]
    steps_here, seq_max, piece_width = embeds.shape
    row_width = norm_gain.shape[1]
    leaves_here = cache_len.shape[0]
    per_leaf = steps_here // leaves_here
    groups = caches.shape[3] // (2 * HD)
    group_size = HQ // KVH
    part_count = lax.axis_size("dp")
    dp_index = lax.axis_index("dp")
    tensor_count = lax.axis_size("tensor")
    tensor_index = lax.axis_index("tensor")
    per_peer = steps_here // part_count
    total_steps = leaf_of_step.shape[0]

    own = embeds.reshape(steps_here * seq_max, piece_width)
    width = (group_size + 2) * HD
    gathered = lax.all_gather(qkv_weight[0], "dp", axis=0, tiled=True)
    local_rows = jnp.zeros((steps_here * seq_max, row_width), own.dtype)
    for shift in range(tensor_count):
        source = lax.rem(tensor_index + tensor_count - shift, tensor_count)
        piece = own
        if shift:
            hops = [(i, (i + shift) % tensor_count) for i in range(tensor_count)]
            piece = lax.ppermute(own, "tensor", hops)
        local_rows = lax.dynamic_update_slice_in_dim(
            local_rows, piece, source * piece_width, 1
        )

    local_ids = jnp.arange(steps_here, dtype=jnp.int32)
    owners = (leaf_of_step // leaves_here).reshape(part_count, steps_here)
    send_orders = jnp.argsort(owners * steps_here + local_ids[None, :], axis=1)
    send_order = lax.dynamic_index_in_dim(send_orders, dp_index, 0, keepdims=False)
    sources = jnp.arange(part_count, dtype=jnp.int32)[:, None] * steps_here
    arriving = (
        lax.dynamic_slice_in_dim(send_orders, dp_index * per_peer, per_peer, 1) + sources
    ).reshape(steps_here)
    arrive_leaf = leaf_of_step[arriving] - dp_index * leaves_here
    arrange = jnp.argsort(arrive_leaf * total_steps + arriving).astype(jnp.int32)
    lengths = step_len[arriving[arrange]]

    as_float = local_rows.astype(jnp.float32)
    inverse_rms = lax.rsqrt(jnp.mean(as_float * as_float, axis=-1, keepdims=True) + norm_eps)
    normed = (as_float * inverse_rms * norm_gain[0]).astype(jnp.bfloat16)

    normed = lax.optimization_barrier(normed)
    contexts, partial_value = None, 0.0
    after = [(arrange, lengths), ()]
    for g in range(groups):
        weight = gathered[:, g * width : (g + 1) * width]
        summed = jnp.dot(normed, weight, preferred_element_type=jnp.float32)
        outbound = summed.astype(jnp.bfloat16).reshape(steps_here, seq_max, width)
        outbound = permute_steps(send_order, outbound, after[g])
        outbound = outbound.reshape(part_count, per_peer, seq_max, width)
        arrived = lax.all_to_all(outbound, "dp", split_axis=0, concat_axis=0, tiled=True)
        arrived = arrived.reshape(steps_here, seq_max, width)
        contexts, shares = attend(
            g, groups, per_leaf, arrange, lengths, cache_len, arrived, caches, score_weight, contexts
        )
        after.append((shares,))
        partial_value = partial_value + jnp.sum(shares, axis=-1)
    model_weight = jnp.where(lax.axis_index("mp") == 0, prior_weight, 1.0).astype(jnp.float32)
    step_value = partial_value * model_weight
    for axis in ("tensor", "mp"):
        step_value = sum_over(step_value, axis)
    return (contexts, step_value)


def solution(mesh):
    placed = (
        P("mp", "dp", None, "tensor"),
        P(),
        P(),
        P("dp"),
        P("mp", "dp", None, "tensor"),
        P("mp", None),
        P("mp", "dp", "tensor"),
        P("mp", "tensor"),
    )
    return jax.shard_map(
        per_device,
        mesh=mesh,
        in_specs=placed,
        out_specs=(P("mp", "dp", None, None, "tensor"), P("dp", None)),
        check_vma=False,
    )
```

```python
import functools

import jax
import jax.numpy as jnp
from jax import lax
from jax.experimental import pallas as pl
from jax.experimental.pallas import tpu as pltpu
from jax.sharding import PartitionSpec as P

KVH = 8
HD = 128
HQ = 32


prior_weight = 0.5
norm_eps = 1e-05


def permute_kernel(order_ref, rows_ref, *refs):
    out_ref = refs[-1]

    def move(slot, carry):
        out_ref[slot] = rows_ref[order_ref[slot]]
        return carry

    lax.fori_loop(0, out_ref.shape[0], move, 0)


def permute_steps(order, rows, after):
    size = rows.size * rows.dtype.itemsize
    return pl.pallas_call(
        permute_kernel,
        out_shape=jax.ShapeDtypeStruct(rows.shape, rows.dtype),
        in_specs=[
            pl.BlockSpec(memory_space=pltpu.SMEM),
            pl.BlockSpec(memory_space=pltpu.VMEM),
        ]
        + [pl.BlockSpec(memory_space=pl.ANY)] * len(after),
        out_specs=pl.BlockSpec(memory_space=pltpu.VMEM),
        compiler_params=pltpu.CompilerParams(vmem_limit_bytes=2 * size + (4 << 20)),
        cost_estimate=pl.CostEstimate(flops=0, bytes_accessed=2 * size, transcendentals=0),
    )(order, rows, *after)


def attend_kernel(
    per_leaf,
    group_size,
    arrange_ref,
    length_ref,
    live_ref,
    rows_ref,
    cache_ref,
    weight_ref,
    *refs,
):
    out_ref, score_ref, query_s, key_s, value_s = refs[-5:]
    leaf = pl.program_id(0)
    seq_max = rows_ref.shape[1]
    cache_rows = cache_ref.shape[2]
    steps_tile = query_s.shape[1] // seq_max
    tile = steps_tile * seq_max
    keys = cache_rows + tile
    key_s[:cache_rows] = cache_ref[0, 0, :, :HD]
    value_s[:cache_rows] = cache_ref[0, 0, :, HD:]
    row = lax.broadcasted_iota(jnp.int32, (tile, keys), 0)
    column = lax.broadcasted_iota(jnp.int32, (tile, keys), 1)
    own = column - cache_rows
    first = row - lax.rem(row, seq_max)
    far_ok = column < jnp.minimum(live_ref[leaf], cache_rows)
    own_ok = (own >= first) & (own <= row)
    bias = jnp.where(far_ok | own_ok, 0.0, -jnp.inf)
    token = lax.broadcasted_iota(jnp.int32, (seq_max, HD), 0)
    scale_q = HD ** (-0.5)
    for part in range(per_leaf // steps_tile):
        valid, last = [], []
        for place in range(steps_tile):
            slot = leaf * per_leaf + part * steps_tile + place
            step = arrange_ref[slot]
            span = pl.ds(place * seq_max, seq_max)
            for head in range(group_size):
                query_s[head, span] = rows_ref[step, :, head * HD : (head + 1) * HD]
            key_s[pl.ds(cache_rows + place * seq_max, seq_max)] = rows_ref[
                step, :, group_size * HD : (group_size + 1) * HD
            ]
            value_s[pl.ds(cache_rows + place * seq_max, seq_max)] = rows_ref[
                step, :, (group_size + 1) * HD : (group_size + 2) * HD
            ]
            valid.append(token < length_ref[slot])
            last.append((token == length_ref[slot] - 1).astype(jnp.float32))
        step_score = [jnp.zeros((1, HD), jnp.float32) for _ in range(steps_tile)]
        for head in range(group_size):
            scores = lax.dot_general(
                query_s[head],
                key_s[...],
                (((1,), (1,)), ((), ())),
                preferred_element_type=jnp.float32,
            )
            scores = scores * scale_q + bias
            probs = jnp.exp(scores - scores.max(-1, keepdims=True))
            total = probs.sum(-1, keepdims=True)
            context = jnp.dot(
                probs.astype(jnp.bfloat16), value_s[...], preferred_element_type=jnp.float32
            )
            context = context / total
            for place in range(steps_tile):
                piece = jnp.where(
                    valid[place], context[place * seq_max : (place + 1) * seq_max], 0.0
                )
                out_ref[0, 0, part * steps_tile + place, :, head * HD : (head + 1) * HD] = (
                    piece.astype(jnp.bfloat16)
                )
                step_score[place] += (piece * last[place]).sum(0, keepdims=True) * weight_ref[
                    :, head * HD : (head + 1) * HD
                ]
        for place in range(steps_tile):
            score_ref[0, pl.ds(part * steps_tile + place, 1)] = step_score[place]


def attend(group, groups, per_leaf, arrange, lengths, live, rows, caches, weight, contexts):
    steps_here, seq_max, columns = rows.shape
    _, leaves_here, cache_rows, _ = caches.shape
    group_size = HQ // KVH
    tile = 128
    width = group_size * HD
    in_specs = [
        pl.BlockSpec((steps_here, seq_max, columns), lambda l, *_: (0, 0, 0)),
        pl.BlockSpec((1, 1, cache_rows, 2 * HD), lambda l, *_: (0, l, 0, group)),
        pl.BlockSpec((1, width), lambda l, *_: (0, group)),
    ]
    operands = [rows, caches, weight]
    aliases = {}
    if contexts is not None:
        in_specs.append(pl.BlockSpec(memory_space=pl.ANY))
        operands.append(contexts)
        aliases = {6: 0}
    work = steps_here * seq_max * group_size * (cache_rows + tile)
    return pl.pallas_call(
        functools.partial(attend_kernel, per_leaf, group_size),
        grid_spec=pltpu.PrefetchScalarGridSpec(
            num_scalar_prefetch=3,
            grid=(leaves_here,),
            in_specs=in_specs,
            out_specs=[
                pl.BlockSpec(
                    (1, 1, per_leaf, seq_max, width), lambda l, *_: (0, l, 0, 0, group)
                ),
                pl.BlockSpec((1, per_leaf, HD), lambda l, *_: (l, 0, 0)),
            ],
            scratch_shapes=[
                pltpu.VMEM((group_size, tile, HD), jnp.bfloat16),
                pltpu.VMEM((cache_rows + tile, HD), jnp.bfloat16),
                pltpu.VMEM((cache_rows + tile, HD), jnp.bfloat16),
            ],
        ),
        out_shape=[
            jax.ShapeDtypeStruct(
                (1, leaves_here, per_leaf, seq_max, groups * width), jnp.bfloat16
            ),
            jax.ShapeDtypeStruct((leaves_here, per_leaf, HD), jnp.float32),
        ],
        input_output_aliases=aliases,
        compiler_params=pltpu.CompilerParams(vmem_limit_bytes=24 << 20),
        cost_estimate=pl.CostEstimate(
            flops=4 * work * HD, bytes_accessed=8 << 20, transcendentals=work
        ),
    )(arrange, lengths, live, *operands)


def sum_over(value, axis):
    count = lax.axis_size(axis)
    if count & (count - 1):
        return lax.psum(value, axis)
    reach = 1
    while reach < count:
        hops = [(i, i ^ reach) for i in range(count)]
        value = value + lax.ppermute(value, axis, hops)
        reach *= 2
    return value


def per_device(
    step_embeds, step_len, leaf_of_step, cache_len, caches, norm_gain, qkv_weight, score_weight
):
    embeds = step_embeds[0]
    steps_here, seq_max, piece_width = embeds.shape
    row_width = norm_gain.shape[1]
    leaves_here = cache_len.shape[0]
    per_leaf = steps_here // leaves_here
    groups = caches.shape[3] // (2 * HD)
    group_size = HQ // KVH
    part_count = lax.axis_size("dp")
    dp_index = lax.axis_index("dp")
    tensor_count = lax.axis_size("tensor")
    tensor_index = lax.axis_index("tensor")
    per_peer = steps_here // part_count
    total_steps = leaf_of_step.shape[0]

    own = embeds.reshape(steps_here * seq_max, piece_width)
    width = (group_size + 2) * HD
    split = max(groups - 1, 1)
    bounds = [(0, split)] + ([(split, groups)] if split < groups else [])
    gathered = [
        lax.all_gather(
            qkv_weight[0, :, start * width : end * width], "dp", axis=0, tiled=True
        )
        for start, end in bounds
    ]
    local_rows = jnp.zeros((steps_here * seq_max, row_width), own.dtype)
    for shift in range(tensor_count):
        source = lax.rem(tensor_index + tensor_count - shift, tensor_count)
        piece = own
        if shift:
            hops = [(i, (i + shift) % tensor_count) for i in range(tensor_count)]
            piece = lax.ppermute(own, "tensor", hops)
        local_rows = lax.dynamic_update_slice_in_dim(
            local_rows, piece, source * piece_width, 1
        )

    local_ids = jnp.arange(steps_here, dtype=jnp.int32)
    owners = (leaf_of_step // leaves_here).reshape(part_count, steps_here)
    send_orders = jnp.argsort(owners * steps_here + local_ids[None, :], axis=1)
    send_order = lax.dynamic_index_in_dim(send_orders, dp_index, 0, keepdims=False)
    sources = jnp.arange(part_count, dtype=jnp.int32)[:, None] * steps_here
    arriving = (
        lax.dynamic_slice_in_dim(send_orders, dp_index * per_peer, per_peer, 1) + sources
    ).reshape(steps_here)
    arrive_leaf = leaf_of_step[arriving] - dp_index * leaves_here
    arrange = jnp.argsort(arrive_leaf * total_steps + arriving).astype(jnp.int32)
    lengths = step_len[arriving[arrange]]

    as_float = local_rows.astype(jnp.float32)
    inverse_rms = lax.rsqrt(jnp.mean(as_float * as_float, axis=-1, keepdims=True) + norm_eps)
    normed = (as_float * inverse_rms * norm_gain[0]).astype(jnp.bfloat16)

    normed = lax.optimization_barrier(normed)
    contexts, partial_value = None, 0.0
    after = [(arrange, lengths), ()]
    for g in range(groups):
        part = 0 if g < split else 1
        place = g - bounds[part][0]
        weight = gathered[part][:, place * width : (place + 1) * width]
        summed = jnp.dot(normed, weight, preferred_element_type=jnp.float32)
        outbound = summed.astype(jnp.bfloat16).reshape(steps_here, seq_max, width)
        outbound = permute_steps(send_order, outbound, after[g] if g < split else ())
        outbound = outbound.reshape(part_count, per_peer, seq_max, width)
        arrived = lax.all_to_all(outbound, "dp", split_axis=0, concat_axis=0, tiled=True)
        arrived = arrived.reshape(steps_here, seq_max, width)
        contexts, shares = attend(
            g, groups, per_leaf, arrange, lengths, cache_len, arrived, caches, score_weight, contexts
        )
        after.append((shares,))
        partial_value = partial_value + jnp.sum(shares, axis=-1)
    model_weight = jnp.where(lax.axis_index("mp") == 0, prior_weight, 1.0).astype(jnp.float32)
    step_value = partial_value * model_weight
    for axis in ("tensor", "mp"):
        step_value = sum_over(step_value, axis)
    return (contexts, step_value)


def solution(mesh):
    placed = (
        P("mp", "dp", None, "tensor"),
        P(),
        P(),
        P("dp"),
        P("mp", "dp", None, "tensor"),
        P("mp", None),
        P("mp", "dp", "tensor"),
        P("mp", "tensor"),
    )
    return jax.shard_map(
        per_device,
        mesh=mesh,
        in_specs=placed,
        out_specs=(P("mp", "dp", None, None, "tensor"), P("dp", None)),
        check_vma=False,
    )
```
